512 devices in a mesh: section: 16 (over z), dp: 32 (over y, x, core).
Axes of the slice: x: 4, y: 4, z: 16, core: 2. Of those that a mesh axis runs over, the one named last changes fastest.
Arguments:
- acts: bfloat16 [16, 16384, 2048], P('section', 'dp'), may hold values from -24 to 24
- key_grads: bfloat16 [16, 16384, 512], P('section', 'dp'), may hold values from -0.013531647 to 0.013531647
- key_weight: bfloat16 [16, 2048, 512], P('section', 'dp'), may hold values from -0.25 to 0.25
- lengths: int32 [32, 16], P('dp'), may hold values from 1 to 128, as said below
- threshold: float32 [], replicated, may hold values from 8 to 24
Outputs:
- act_grad: bfloat16 [16, 16384, 2048], P('section', 'dp')
- weight_grad: float32 [16, 2048, 512], P('section', 'dp')
The draws below stay inside these ranges and needn't reach their ends.
Inputs may be any that keep to these rules, and one draw needn't show every extreme that they name: `lengths`: each row sums to 512, and its longest patient has exactly 128 tokens.
All inputs are finite; a program needn't handle non-finite values.
Results may differ from the reference program's by a relative error of at most 0.002.
Values may be sent and summed in bfloat16 or wider, within the bound.
A program may use at most 64 MiB of HBM per device.

```python
import jax
import jax.numpy as jnp
from jax import lax

D = 2048
KV = 512
PAT_DEV = 16
LMAX = 128
TOK_DEV = 512
LAYERS = 16
TOKENS = 16384
PATIENTS = 512
N_DP = 32


def timelines(key):
    key = jax.random.fold_in(key, 101)
    first, second = jax.random.split(key)
    weights = jax.random.randint(first, (N_DP, PAT_DEV), 1, 17).astype(jnp.int32)
    weights = weights * weights
    longest = jax.random.randint(second, (N_DP,), 0, PAT_DEV).astype(jnp.int32)
    column = jnp.arange(PAT_DEV, dtype=jnp.int32)
    is_long = column[None, :] == longest[:, None]
    weights = jnp.where(is_long, 0, weights)
    spare = TOK_DEV - LMAX - (PAT_DEV - 1)
    limit = LMAX - 1
    total_weight = jnp.maximum(jnp.sum(weights, axis=1, keepdims=True), 1)
    extra = jnp.minimum(spare * weights // total_weight, limit)
    extra = jnp.where(is_long, 0, extra)
    room = jnp.where(is_long, 0, limit - extra)
    left = spare - jnp.sum(extra, axis=1, keepdims=True)
    before = jnp.cumsum(room, axis=1) - room
    extra = extra + jnp.clip(left - before, 0, room)
    lengths = jnp.where(is_long, LMAX, 1 + extra).astype(jnp.int32)
    ends = jnp.cumsum(lengths, axis=1)
    position = jnp.arange(TOK_DEV, dtype=jnp.int32)
    local = jnp.sum((position[None, :, None] >= ends[:, None, :]).astype(jnp.int32), axis=2)
    owner = jnp.arange(N_DP, dtype=jnp.int32)[:, None] * PAT_DEV + local
    return (lengths, owner.reshape(TOKENS).astype(jnp.int32))


def draw_lengths(key, part):
    lengths, owner = timelines(key)
    return lengths


def draw_acts(key, part):
    lengths, owner = timelines(key)
    key = jax.random.fold_in(key, 5)
    order = jax.random.permutation(jax.random.fold_in(key, 1), N_DP)
    device_of = jnp.arange(TOKENS, dtype=jnp.int32) // TOK_DEV
    column_block = jnp.arange(D, dtype=jnp.int32) // (D // N_DP)
    boost = jnp.where(order[device_of][:, None] == column_block[None, :], jnp.float32(3.0), jnp.float32(1.0))

    def one_layer(layer):
        layer_key = jax.random.fold_in(key, layer + 2)
        k_shared, k_noise, k_weight = jax.random.split(layer_key, 3)
        strength = jax.random.uniform(k_weight, (PATIENTS,), jnp.float32, 0.25, 0.85)
        shared = jax.random.normal(k_shared, (PATIENTS, D), jnp.float32)
        noise = jax.random.normal(k_noise, (TOKENS, D), jnp.float32)
        value = strength[owner][:, None] * shared[owner] + noise
        value = jnp.clip(value, -8.0, 8.0) * boost
        return value.astype(jnp.bfloat16)
    return lax.map(one_layer, jnp.arange(LAYERS, dtype=jnp.int32))


def draw_key_grads(key, part):
    lengths, owner = timelines(key)
    key = jax.random.fold_in(key, 7)
    level = jnp.arange(LAYERS, dtype=jnp.float32)
    amplitude = jnp.sqrt(1.0 + 2.0 * level / max(LAYERS - 1, 1)) * (D * KV) ** (-0.5)

    def one_layer(layer):
        layer_key = jax.random.fold_in(key, layer + 2)
        k_shared, k_noise, k_weight = jax.random.split(layer_key, 3)
        strength = jax.random.uniform(k_weight, (PATIENTS,), jnp.float32, 0.25, 0.85)
        shared = jax.random.normal(k_shared, (PATIENTS, KV), jnp.float32)
        noise = jax.random.normal(k_noise, (TOKENS, KV), jnp.float32)
        value = strength[owner][:, None] * shared[owner] + noise
        value = jnp.clip(value, -8.0, 8.0) * amplitude[layer]
        return value.astype(jnp.bfloat16)
    return lax.map(one_layer, jnp.arange(LAYERS, dtype=jnp.int32))


def block_scale(key, shape, pieces, least, largest):
    gain = 1.0
    for axis_at, parts in pieces:
        draws = jax.random.uniform(jax.random.fold_in(jax.random.fold_in(key, 6), axis_at), (parts,), jnp.float32, least / len(pieces), largest / len(pieces))
        gain = gain * jnp.repeat(jnp.exp(draws), shape[axis_at] // parts).reshape((-1,) + (1,) * (len(shape) - 1 - axis_at))
    return gain


def gaussian(stream_key, shape, scale, reach, pieces=(), held_as=jnp.bfloat16):
    entries = jax.random.normal(stream_key, shape, jnp.float32) * scale
    if len(pieces) > 0:
        entries = block_scale(stream_key, shape, pieces, -0.22, 0.18) * entries
    return jnp.clip(entries, min=-reach, max=reach).astype(held_as)


def setup_inputs(seed: int = 0) -> dict:
    keys = jax.random.split(jax.random.key(seed), 6)
    acts = draw_acts(jax.random.fold_in(keys[5], 71), 0)
    key_grads = draw_key_grads(jax.random.fold_in(keys[5], 71), 0)
    key_weight = gaussian(keys[2], (LAYERS, D, KV), KV ** -0.5, 0.25, ((0, 16), (1, 32)))
    lengths = draw_lengths(jax.random.fold_in(keys[5], 71), 0)
    threshold = jnp.clip(jax.random.uniform(keys[4], (), jnp.float32, 8.0, 24.0), 8.0, 24.0)
    return {"acts": acts, "key_grads": key_grads, "key_weight": key_weight, "lengths": lengths, "threshold": threshold}


def segment_of(lengths_row):
    ends = jnp.cumsum(lengths_row)
    position = jnp.arange(TOK_DEV, dtype=jnp.int32)
    return lax.optimization_barrier(jnp.sum((position[:, None] >= ends[None, :]).astype(jnp.int32), axis=1)).astype(jnp.int32)

def banded_norms(inputs, grads, seg):
    count = TOK_DEV // LMAX
    xr = inputs.astype(jnp.float32).reshape(count, LMAX, D)
    gr = grads.astype(jnp.float32).reshape(count, LMAX, KV)
    xn = jnp.concatenate([xr[1:], jnp.zeros((1, LMAX, D), jnp.float32)], axis=0)
    gn = jnp.concatenate([gr[1:], jnp.zeros((1, LMAX, KV), jnp.float32)], axis=0)
    sr = seg.reshape(count, LMAX)
    sn = jnp.concatenate([sr[1:], jnp.full((1, LMAX), -1, jnp.int32)], axis=0)
    inner = jnp.einsum('btd,bud->btu', xr, xr) * jnp.einsum('btd,bud->btu', gr, gr)
    outer = jnp.einsum('btd,bud->btu', xr, xn) * jnp.einsum('btd,bud->btu', gr, gn)
    inner = jnp.where(sr[:, :, None] == sr[:, None, :], inner, jnp.float32(0.0))
    outer = jnp.where(sr[:, :, None] == sn[:, None, :], outer, jnp.float32(0.0))
    rowsum = lax.optimization_barrier(jnp.sum(inner, axis=2)) + 2.0 * lax.optimization_barrier(jnp.sum(outer, axis=2))
    patient = jnp.arange(PAT_DEV, dtype=jnp.int32)
    onehot = sr[:, :, None] == patient[None, None, :]
    return lax.optimization_barrier(jnp.sum(jnp.where(onehot, rowsum[:, :, None], jnp.float32(0.0)), axis=(0, 1)))

def reference(acts, key_grads, key_weight, lengths, threshold):
    seg = jax.vmap(segment_of)(lengths)

    def layer_sq(layer):
        inputs = acts[layer].reshape(N_DP, TOK_DEV, D)
        grads = key_grads[layer].reshape(N_DP, TOK_DEV, KV)
        return jax.vmap(banded_norms)(inputs, grads, seg)
    squares = lax.map(layer_sq, jnp.arange(LAYERS))
    norm = jnp.sqrt(lax.optimization_barrier(jnp.sum(squares, axis=0)))
    factor = threshold / jnp.maximum(norm, threshold)
    token_factor = jnp.take_along_axis(factor, seg, axis=1).reshape(TOKENS)

    def layer_out(layer):
        scaled = (key_grads[layer].astype(jnp.float32) * token_factor[:, None]).astype(jnp.bfloat16)
        weight_part = jnp.dot(acts[layer].T, scaled, preferred_element_type=jnp.float32)
        act_part = jnp.dot(key_grads[layer], key_weight[layer].T, preferred_element_type=jnp.float32).astype(jnp.bfloat16)
        return (act_part, weight_part)
    act_grad, weight_grad = lax.map(layer_out, jnp.arange(LAYERS))
    return (act_grad, weight_grad)
```

```python
import jax
import jax.numpy as jnp
from jax import lax
from jax.experimental import pallas as pl
from jax.experimental.pallas import tpu as pltpu
from jax.sharding import PartitionSpec as P

MESH = pl.DeviceIdType.MESH
F32, BF16 = jnp.float32, jnp.bfloat16
NT = (((1,), (1,)), ((), ()))
D, KV, TOK, PAT = 2048, 512, 512, 16
POS = {2: 0, 1: 1, 3: 2, 0: 3}
GROUPS = ((0, 1), (1, 3), (3, 4))
N_SEMS = 108


def kernel(
    acts_hbm, kg_hbm, w_hbm, len_ref, thr_ref, act_out, wg_out,
    acts, kg, kgs, kgt, sct, wr, act_v,
    zv, zr, z2s, z2r, z9s, z9r,
    pb, pc, pf, ra, cb, rx, ss, ra2, cb2, rx2, tb, wsw,
    ssem, rsem, lsem,
):
    z = lax.axis_index("section")
    dp = lax.axis_index("dp")
    core = lax.rem(dp, 2)
    xx = lax.rem(lax.div(dp, 2), 4)
    yy = lax.div(dp, 8)

    def dev(dy=0, dx=0, dc=0, dz=0):
        y2, x2 = lax.rem(yy + dy + 4, 4), lax.rem(xx + dx + 4, 4)
        c2 = 1 - core if dc else core
        return (lax.rem(z + dz + 16, 16), (y2 * 4 + x2) * 2 + c2)

    started = []

    def send(src, dst, to):
        k = len(started)
        copy = pltpu.make_async_remote_copy(
            src_ref=src, dst_ref=dst, send_sem=ssem.at[k], recv_sem=rsem.at[k],
            device_id=to, device_id_type=MESH,
        )
        copy.start()
        started.append(copy)
        return copy

    load_kg = pltpu.make_async_copy(kg_hbm, kg, lsem.at[0])
    load_acts = pltpu.make_async_copy(acts_hbm, acts.at[0], lsem.at[1])
    load_w = pltpu.make_async_copy(w_hbm, wr.at[0, 0, core], lsem.at[2])
    load_kg.start()
    load_acts.start()
    load_w.start()

    near = [dev(dc=1), dev(dx=1), dev(dx=-1), dev(dy=1), dev(dy=-1)]
    zs = [1, -1, 2, -2, 3, -3, 4, -4]
    partners = near + [dev(dz=k) for k in zs] + [dev(dz=4, dc=1), dev(dz=-4, dc=1)]
    barrier = pltpu.get_barrier_semaphore()
    for who in partners:
        pl.semaphore_signal(barrier, inc=1, device_id=who, device_id_type=MESH)

    lane = lax.broadcasted_iota(jnp.int32, (1, TOK), 1)
    sub = lax.broadcasted_iota(jnp.int32, (TOK, 1), 0)
    seg_row = jnp.zeros((1, TOK), jnp.int32)
    seg_col = jnp.zeros((TOK, 1), jnp.int32)
    end = jnp.int32(0)
    for p in range(PAT):
        end = end + len_ref[0, p]
        seg_row = seg_row + (lane >= end).astype(jnp.int32)
        seg_col = seg_col + (sub >= end).astype(jnp.int32)

    load_kg.wait()
    load_acts.wait()

    def masked(rows, cols):
        (r0, r1), (c0, c1) = rows, cols
        gx = lax.dot_general(acts[0, r0:r1], acts[0, c0:c1], NT, preferred_element_type=F32)
        gg = lax.dot_general(kg[r0:r1], kg[c0:c1], NT, preferred_element_type=F32)
        same = seg_col[r0:r1] == seg_row[:, c0:c1]
        return same, jnp.sum(jnp.where(same, gx * gg, 0.0), axis=1, keepdims=True)

    def spread(same, r):
        return jnp.sum(jnp.where(same, r, 0.0), axis=0, keepdims=True)

    same_a, r_a = masked((0, 256), (0, 256))
    same_c, r_c = masked((128, 256), (256, 384))
    same_b, r_b = masked((256, 512), (256, 512))
    r_1 = r_a[128:] + 2.0 * r_c
    same_t = seg_col[256:384] == seg_row[:, 128:256]
    v_a = spread(same_a[:128], r_a[:128]) + spread(same_a[128:], r_1)
    v_b = spread(same_b, r_b)
    zv[:, 0:128] = v_a[:, 0:128]
    zv[:, 128:256] = v_a[:, 128:256] + spread(same_t, r_b[:128])
    zv[:, 256:384] = v_b[:, 0:128] + spread(same_c, r_1)
    zv[:, 384:512] = v_b[:, 128:256]

    pl.semaphore_wait(barrier, len(partners))

    z1 = [send(zv, zr.at[i], dev(dz=k)) for i, k in enumerate(zs)]

    load_w.wait()
    step = (lambda s: dev(dx=s), lambda s: dev(dy=s))

    def at(h, d1, d2):
        return (d2, d1) if h == 0 else (d1, d2)

    def slot(h, d1, d2, lo=0, hi=32):
        return wr.at[(*at(h, d1, d2), core, pl.ds(32 * h + lo, hi - lo))]

    g_a1, g_a2, g_b1, g_b2 = {}, {}, {}, {}
    for h in range(2):
        g_a1[h] = (
            send(slot(h, 0, 0), slot(h, 3, 0), step[h](1)),
            send(slot(h, 0, 0), slot(h, 1, 0), step[h](-1)),
        )
    share_kg = send(
        kg.at[:, pl.ds(pl.multiple_of(256 * (1 - core), 256), 256)], kgs, dev(dc=1)
    )
    share_acts = send(acts.at[0], acts.at[1], dev(dc=1))

    def second(h, d1):
        return (
            send(slot(h, d1, 0), slot(h, d1, 3), step[1 - h](1)),
            send(slot(h, d1, 0), slot(h, d1, 1), step[1 - h](-1)),
        )

    def second_forward(h, d1):
        for c in g_b1[h, d1]:
            c.wait_recv()
        g_b2[h, d1] = (
            send(slot(h, d1, 3, 0, 16), slot(h, d1, 2, 0, 16), step[1 - h](1)),
            send(slot(h, d1, 1, 16, 32), slot(h, d1, 2, 16, 32), step[1 - h](-1)),
        )

    for h in range(2):
        g_b1[h, 0] = second(h, 0)

    own = pl.multiple_of(256 * core, 256)
    kgt[:, 0:512] = kg[:, pl.ds(own, 256)].T

    for h in range(2):
        for c in g_a1[h]:
            c.wait_recv()
        g_a2[h] = (
            send(slot(h, 3, 0, 0, 16), slot(h, 2, 0, 0, 16), step[h](1)),
            send(slot(h, 1, 0, 16, 32), slot(h, 2, 0, 16, 32), step[h](-1)),
        )
    for h in range(2):
        for d1 in (1, 3):
            g_b1[h, d1] = second(h, d1)
    for h in range(2):
        for c in g_a2[h]:
            c.wait_recv()
        g_b1[h, 2] = second(h, 2)
        second_forward(h, 0)

    share_kg.wait_recv()
    kgt[:, 512:1024] = kgs[...].T

    for c in z1:
        c.wait_recv()
    up = zr[0] + zr[2] + zr[4]
    down = zr[1] + zr[3] + zr[5]
    z2s[0] = up + zr[6]
    z2s[1] = down
    nine = zv[...] + (up + down) + (zr[6] + zr[7])
    z9s[...] = nine
    z2 = [
        send(z2s.at[0], z2r.at[0, 0], dev(dz=4)),
        send(z2s.at[1], z2r.at[0, 1], dev(dz=-4)),
        send(z2s.at[0], z2r.at[1, 0], dev(dz=4, dc=1)),
        send(z2s.at[1], z2r.at[1, 1], dev(dz=-4, dc=1)),
        send(z9s, z9r, dev(dc=1)),
    ]

    for d1 in (1, 3):
        for h in range(2):
            second_forward(h, d1)
    for h in range(2):
        second_forward(h, 2)

    for c in z2:
        c.wait_recv()
    thr = thr_ref[0, 0]
    for s, total in ((0, nine + (z2r[0, 0] + z2r[0, 1])), (1, z9r[...] + (z2r[1, 0] + z2r[1, 1]))):
        factor = thr / jnp.maximum(jnp.sqrt(total), thr)
        cols = slice(512 * s, 512 * s + 512)
        sct[:, cols] = (kgt[:, cols].astype(F32) * factor).astype(BF16)
    share_acts.wait_recv()

    def chip(dy, dx):
        return lax.rem(yy + dy, 4) * 4 + lax.rem(xx + dx, 4)

    def columns(dy, dx):
        return pl.ds(pl.multiple_of(128 * chip(dy, dx), 128), 128)

    def product(pair):
        out = None
        for s in range(2):
            rhs = jnp.concatenate([acts[s, :, columns(*q)] for q in pair], axis=1)
            part = jnp.dot(sct[:, 512 * s : 512 * s + 512], rhs, preferred_element_type=F32)
            out = part if out is None else out + part
        for i, (dy, dx) in enumerate(pair):
            for h in range(2):
                d1, d2 = (dx, dy) if h == 0 else (dy, dx)
                r = out[128 * h : 128 * h + 128, 128 * i : 128 * i + 128]
                p = POS[d2]
                if d1 == 0:
                    pf[h, p] = r
                elif d1 == 2:
                    pb[h, 1, p] = r.astype(BF16)
                elif d1 == 1:
                    pc[h, 0, p] = r[:64]
                    pb[h, 0, p, 64:] = r[64:].astype(BF16)
                else:
                    pb[h, 2, p, :64] = r[:64].astype(BF16)
                    pc[h, 1, p] = r[64:]

    s_a, s_b, s_c = {}, {}, {}

    def send_a(g):
        lo, hi = GROUPS[g]
        ps = pl.ds(lo, hi - lo)
        for h in range(2):
            s_a[h, g] = (
                send(pb.at[h, 1, ps, pl.ds(0, 64)], ra.at[h, 0, ps], step[h](1)),
                send(pb.at[h, 1, ps, pl.ds(64, 64)], ra.at[h, 1, ps], step[h](-1)),
            )

    def send_b(g):
        lo, hi = GROUPS[g]
        ps = pl.ds(lo, hi - lo)
        for h in range(2):
            s_b[h, g] = (
                send(pb.at[h, 0, ps, pl.ds(64, 64)], rx.at[h, 0, ps, pl.ds(64, 64)], step[h](1)),
                send(pb.at[h, 2, ps, pl.ds(0, 64)], rx.at[h, 1, ps, pl.ds(0, 64)], step[h](-1)),
            )

    def send_c(g):
        lo, hi = GROUPS[g]
        ps = pl.ds(lo, hi - lo)
        for h in range(2):
            pair = []
            for s in range(2):
                s_a[h, g][s].wait_recv()
                for p in range(lo, hi):
                    cb[h, s, p] = (pc[h, s, p] + ra[h, s, p].astype(F32)).astype(BF16)
                pair.append(
                    send(cb.at[h, s, ps], rx.at[h, s, ps, pl.ds(64 * s, 64)], step[h](1 - 2 * s))
                )
            s_c[h, g] = pair

    def gathered(g):
        lo, hi = GROUPS[g]
        for h in range(2):
            for s in range(2):
                s_b[h, g][s].wait_recv()
                s_c[h, g][s].wait_recv()
            for p in range(lo, hi):
                ss[h, p] = pf[h, p] + rx[h, 0, p].astype(F32) + rx[h, 1, p].astype(F32)

    product(((2, 2), (2, 1)))
    product(((2, 3), (1, 2)))
    send_a(0)
    product(((3, 2), (1, 1)))
    send_b(0)
    send_a(1)
    product(((1, 3), (3, 1)))
    product(((3, 3), (0, 2)))
    send_b(1)
    product(((2, 0), (0, 1)))
    send_a(2)
    product(((0, 3), (1, 0)))
    product(((3, 0), (0, 0)))
    send_b(2)
    send_c(0)

    for h in range(2):
        for d1 in range(4):
            for c in g_b2[h, d1]:
                c.wait_recv()
    share_w = [
        send(wr.at[dy, :, core], wr.at[dy, :, core], dev(dc=1)) for dy in range(4)
    ]

    send_c(1)
    gathered(0)
    p2a = [
        (
            send(ss.at[h, 0, pl.ds(0, 64)], ra2.at[h, 0], step[1 - h](1)),
            send(ss.at[h, 0, pl.ds(64, 64)], ra2.at[h, 1], step[1 - h](-1)),
        )
        for h in range(2)
    ]
    send_c(2)

    def act_rows(dy):
        share_w[dy].wait_recv()
        for dx in (0, 2):
            w = wr[dy, dx : dx + 2].reshape(256, KV)
            out = lax.dot_general(kg[...], w, NT, preferred_element_type=F32).astype(BF16)
            act_v[:, columns(dy, dx)] = out[:, :128]
            act_v[:, columns(dy, dx + 1)] = out[:, 128:]

    act_rows(0)
    act_rows(1)

    gathered(1)
    p2b = [
        (
            send(ss.at[h, 1, pl.ds(64, 64)], rx2.at[h, 0, pl.ds(64, 64)], step[1 - h](1)),
            send(ss.at[h, 2, pl.ds(0, 64)], rx2.at[h, 1, pl.ds(0, 64)], step[1 - h](-1)),
        )
        for h in range(2)
    ]
    p2c = []
    for h in range(2):
        for s in range(2):
            p2a[h][s].wait_recv()
            cb2[h, s] = ss[h, 1 + s, 64 * s : 64 * s + 64] + ra2[h, s]
            p2c.append(send(cb2.at[h, s], rx2.at[h, s, pl.ds(64 * s, 64)], step[1 - h](1 - 2 * s)))

    act_rows(2)
    act_rows(3)
    store = pltpu.make_async_copy(act_v, act_out, lsem.at[3])
    store.start()

    gathered(2)
    for h in range(2):
        for s in range(2):
            p2b[h][s].wait_recv()
            p2c[2 * h + s].wait_recv()
        tb[:, 128 * h : 128 * h + 128] = (ss[h, 3] + rx2[h, 0] + rx2[h, 1]).T
    swap = send(tb.at[pl.ds(pl.multiple_of(64 * (1 - core), 64), 64)], wsw, dev(dc=1))
    wg_out[:, pl.ds(own, 256)] = tb[pl.ds(pl.multiple_of(64 * core, 64), 64)]
    swap.wait_recv()
    wg_out[:, pl.ds(pl.multiple_of(256 * (1 - core), 256), 256)] = wsw[...]
    store.wait()
    assert len(started) == N_SEMS
    for c in started:
        c.wait_send()


def shards(acts, key_grads, key_weight, lengths, threshold):
    hbm = pl.BlockSpec(memory_space=pl.ANY)
    smem = pl.BlockSpec(memory_space=pltpu.SMEM)
    v = pltpu.VMEM
    act_part, weight_part = pl.pallas_call(
        kernel,
        out_shape=(
            jax.ShapeDtypeStruct((TOK, D), BF16),
            jax.ShapeDtypeStruct((D // 32, KV), F32),
        ),
        in_specs=[hbm, hbm, hbm, smem, smem],
        out_specs=(hbm, pl.BlockSpec(memory_space=v)),
        scratch_shapes=[
            v((2, TOK, D), BF16),
            v((TOK, KV), BF16),
            v((TOK, 256), BF16),
            v((256, 2 * TOK), BF16),
            v((256, 2 * TOK), BF16),
            v((4, 4, 2, 64, KV), BF16),
            v((TOK, D), BF16),
            v((1, TOK), F32),
            v((8, 1, TOK), F32),
            v((2, 1, TOK), F32),
            v((2, 2, 1, TOK), F32),
            v((1, TOK), F32),
            v((1, TOK), F32),
            v((2, 3, 4, 128, 128), BF16),
            v((2, 2, 4, 64, 128), F32),
            v((2, 4, 128, 128), F32),
            v((2, 2, 4, 64, 128), BF16),
            v((2, 2, 4, 64, 128), BF16),
            v((2, 2, 4, 128, 128), BF16),
            v((2, 4, 128, 128), F32),
            v((2, 2, 64, 128), F32),
            v((2, 2, 64, 128), F32),
            v((2, 2, 128, 128), F32),
            v((128, 256), F32),
            v((64, 256), F32),
            pltpu.SemaphoreType.DMA((N_SEMS,)),
            pltpu.SemaphoreType.DMA((N_SEMS,)),
            pltpu.SemaphoreType.DMA((4,)),
        ],
        compiler_params=pltpu.CompilerParams(
            collective_id=0, has_side_effects=True, vmem_limit_bytes=48 * 2**20
        ),
    )(acts[0], key_grads[0], key_weight[0], lengths, threshold.reshape(1, 1))
    return (act_part[None], weight_part[None])


def solution(mesh):
    in_specs = (
        P("section", "dp", None),
        P("section", "dp", None),
        P("section", "dp", None),
        P("dp", None),
        P(),
    )
    out_specs = (P("section", "dp", None), P("section", "dp", None))
    return jax.shard_map(shards, mesh=mesh, in_specs=in_specs, out_specs=out_specs, check_vma=False)
```

```python
import jax
import jax.numpy as jnp
from jax import lax
from jax.experimental import pallas as pl
from jax.experimental.pallas import tpu as pltpu
from jax.sharding import PartitionSpec as P

MESH = pl.DeviceIdType.MESH
F32, BF16 = jnp.float32, jnp.bfloat16
NT = (((1,), (1,)), ((), ()))
D, KV, TOK, PAT = 2048, 512, 512, 16
POS = {2: 0, 1: 1, 3: 2, 0: 3}
GROUPS = ((0, 1), (1, 3), (3, 4))
N_SEMS = 108


def kernel(
    acts_hbm, kg_hbm, w_hbm, len_ref, thr_ref, act_out, wg_out,
    acts, kg, kgs, kgt, sct, wr, act_v,
    zv, zr, z2s, z2r, z9s, z9r,
    pb, pc, pf, ra, cb, rx, ss, ra2, cb2, rx2, tb, wsw,
    ssem, rsem, lsem,
):
    z = lax.axis_index("section")
    dp = lax.axis_index("dp")
    core = lax.rem(dp, 2)
    xx = lax.rem(lax.div(dp, 2), 4)
    yy = lax.div(dp, 8)

    def dev(dy=0, dx=0, dc=0, dz=0):
        y2, x2 = lax.rem(yy + dy + 4, 4), lax.rem(xx + dx + 4, 4)
        c2 = 1 - core if dc else core
        return (lax.rem(z + dz + 16, 16), (y2 * 4 + x2) * 2 + c2)

    started = []

    def send(src, dst, to):
        k = len(started)
        copy = pltpu.make_async_remote_copy(
            src_ref=src, dst_ref=dst, send_sem=ssem.at[k], recv_sem=rsem.at[k],
            device_id=to, device_id_type=MESH,
        )
        copy.start()
        started.append(copy)
        return copy

    load_kg = pltpu.make_async_copy(kg_hbm, kg, lsem.at[0])
    load_lo = pltpu.make_async_copy(acts_hbm.at[0:256], acts.at[0, 0:256], lsem.at[1])
    load_hi = pltpu.make_async_copy(acts_hbm.at[256:512], acts.at[0, 256:512], lsem.at[2])
    load_w = pltpu.make_async_copy(w_hbm, wr.at[0, 0, core], lsem.at[3])
    load_kg.start()
    load_lo.start()
    load_hi.start()
    load_w.start()

    near = [dev(dc=1), dev(dx=1), dev(dx=-1), dev(dy=1), dev(dy=-1)]
    zs = [1, -1, 2, -2, 3, -3, 4, -4]
    partners = near + [dev(dz=k) for k in zs] + [dev(dz=4, dc=1), dev(dz=-4, dc=1)]
    barrier = pltpu.get_barrier_semaphore()
    for who in partners:
        pl.semaphore_signal(barrier, inc=1, device_id=who, device_id_type=MESH)

    pl.semaphore_wait(barrier, len(partners))

    step = (lambda s: dev(dx=s), lambda s: dev(dy=s))

    def at(h, d1, d2):
        return (d2, d1) if h == 0 else (d1, d2)

    def slot(h, d1, d2, lo=0, hi=32):
        return wr.at[(*at(h, d1, d2), core, pl.ds(32 * h + lo, hi - lo))]

    g_a1, g_a2, g_b1, g_b2 = {}, {}, {}, {}
    for h in range(2):
        mine = w_hbm.at[pl.ds(32 * h, 32)]
        g_a1[h] = (
            send(mine, slot(h, 3, 0), step[h](1)),
            send(mine, slot(h, 1, 0), step[h](-1)),
        )

    def second(h, d1):
        mine = slot(h, d1, 0) if d1 else w_hbm.at[pl.ds(32 * h, 32)]
        return (
            send(mine, slot(h, d1, 3), step[1 - h](1)),
            send(mine, slot(h, d1, 1), step[1 - h](-1)),
        )

    def second_forward(h, d1):
        for c in g_b1[h, d1]:
            c.wait_recv()
        g_b2[h, d1] = (
            send(slot(h, d1, 3, 0, 16), slot(h, d1, 2, 0, 16), step[1 - h](1)),
            send(slot(h, d1, 1, 16, 32), slot(h, d1, 2, 16, 32), step[1 - h](-1)),
        )

    for h in range(2):
        g_b1[h, 0] = second(h, 0)
    share_kg = send(
        kg_hbm.at[:, pl.ds(pl.multiple_of(256 * (1 - core), 256), 256)], kgs, dev(dc=1)
    )
    share_acts = send(acts_hbm, acts.at[1], dev(dc=1))

    lane = lax.broadcasted_iota(jnp.int32, (1, TOK), 1)
    sub = lax.broadcasted_iota(jnp.int32, (TOK, 1), 0)
    seg_row = jnp.zeros((1, TOK), jnp.int32)
    seg_col = jnp.zeros((TOK, 1), jnp.int32)
    end = jnp.int32(0)
    for p in range(PAT):
        end = end + len_ref[0, p]
        seg_row = seg_row + (lane >= end).astype(jnp.int32)
        seg_col = seg_col + (sub >= end).astype(jnp.int32)


    def masked(rows, cols):
        (r0, r1), (c0, c1) = rows, cols
        gx = lax.dot_general(acts[0, r0:r1], acts[0, c0:c1], NT, preferred_element_type=F32)
        gg = lax.dot_general(kg[r0:r1], kg[c0:c1], NT, preferred_element_type=F32)
        same = seg_col[r0:r1] == seg_row[:, c0:c1]
        return same, jnp.sum(jnp.where(same, gx * gg, 0.0), axis=1, keepdims=True)

    def spread(same, r):
        return jnp.sum(jnp.where(same, r, 0.0), axis=0, keepdims=True)

    load_kg.wait()
    load_lo.wait()
    same_a, r_a = masked((0, 256), (0, 256))
    load_hi.wait()
    same_c, r_c = masked((128, 256), (256, 384))
    same_b, r_b = masked((256, 512), (256, 512))
    r_1 = r_a[128:] + 2.0 * r_c
    same_t = seg_col[256:384] == seg_row[:, 128:256]
    v_a = spread(same_a[:128], r_a[:128]) + spread(same_a[128:], r_1)
    v_b = spread(same_b, r_b)
    zv[:, 0:128] = v_a[:, 0:128]
    zv[:, 128:256] = v_a[:, 128:256] + spread(same_t, r_b[:128])
    zv[:, 256:384] = v_b[:, 0:128] + spread(same_c, r_1)
    zv[:, 384:512] = v_b[:, 128:256]

    z1 = [send(zv, zr.at[i], dev(dz=k)) for i, k in enumerate(zs)]

    own = pl.multiple_of(256 * core, 256)
    kgt[:, 0:512] = kg[:, pl.ds(own, 256)].T

    for h in range(2):
        for c in g_a1[h]:
            c.wait_recv()
        g_a2[h] = (
            send(slot(h, 3, 0, 0, 16), slot(h, 2, 0, 0, 16), step[h](1)),
            send(slot(h, 1, 0, 16, 32), slot(h, 2, 0, 16, 32), step[h](-1)),
        )
    for h in range(2):
        for d1 in (1, 3):
            g_b1[h, d1] = second(h, d1)
    for h in range(2):
        for c in g_a2[h]:
            c.wait_recv()
        g_b1[h, 2] = second(h, 2)
        second_forward(h, 0)

    share_kg.wait_recv()
    kgt[:, 512:1024] = kgs[...].T

    for c in z1[0::2]:
        c.wait_recv()
    up = zr[0] + zr[2] + zr[4] + zr[6]
    z2s[0] = up
    z2 = [
        send(z2s.at[0], z2r.at[0, 0], dev(dz=4)),
        send(z2s.at[0], z2r.at[1, 0], dev(dz=4, dc=1)),
    ]
    for c in z1[1::2]:
        c.wait_recv()
    down = zr[1] + zr[3] + zr[5]
    z2s[1] = down
    z2 += [
        send(z2s.at[1], z2r.at[0, 1], dev(dz=-4)),
        send(z2s.at[1], z2r.at[1, 1], dev(dz=-4, dc=1)),
    ]
    nine = zv[...] + up + (down + zr[7])
    z9s[...] = nine
    z2.append(send(z9s, z9r, dev(dc=1)))

    for d1 in (1, 3):
        for h in range(2):
            second_forward(h, d1)
    for h in range(2):
        second_forward(h, 2)

    load_w.wait()
    for h in range(2):
        for d1 in range(4):
            for c in g_b2[h, d1]:
                c.wait_recv()
    share_w = [
        send(wr.at[dy, :, core], wr.at[dy, :, core], dev(dc=1)) for dy in range(4)
    ]

    for c in z2:
        c.wait_recv()
    thr = thr_ref[0, 0]
    for s, total in ((0, nine + (z2r[0, 0] + z2r[0, 1])), (1, z9r[...] + (z2r[1, 0] + z2r[1, 1]))):
        factor = thr / jnp.maximum(jnp.sqrt(total), thr)
        cols = slice(512 * s, 512 * s + 512)
        sct[:, cols] = (kgt[:, cols].astype(F32) * factor).astype(BF16)
    share_acts.wait_recv()

    def chip(dy, dx):
        return lax.rem(yy + dy, 4) * 4 + lax.rem(xx + dx, 4)

    def columns(dy, dx):
        return pl.ds(pl.multiple_of(128 * chip(dy, dx), 128), 128)

    def product(pair):
        out = None
        for s in range(2):
            rhs = jnp.concatenate([acts[s, :, columns(*q)] for q in pair], axis=1)
            part = jnp.dot(sct[:, 512 * s : 512 * s + 512], rhs, preferred_element_type=F32)
            out = part if out is None else out + part
        for i, (dy, dx) in enumerate(pair):
            for h in range(2):
                d1, d2 = (dx, dy) if h == 0 else (dy, dx)
                r = out[128 * h : 128 * h + 128, 128 * i : 128 * i + 128]
                p = POS[d2]
                if d1 == 0:
                    pf[h, p] = r
                elif d1 == 2:
                    pb[h, 1, p] = r.astype(BF16)
                elif d1 == 1:
                    pc[h, 0, p] = r[:64]
                    pb[h, 0, p, 64:] = r[64:].astype(BF16)
                else:
                    pb[h, 2, p, :64] = r[:64].astype(BF16)
                    pc[h, 1, p] = r[64:]

    s_a, s_b, s_c = {}, {}, {}

    def send_a(g):
        lo, hi = GROUPS[g]
        ps = pl.ds(lo, hi - lo)
        for h in range(2):
            s_a[h, g] = (
                send(pb.at[h, 1, ps, pl.ds(0, 64)], ra.at[h, 0, ps], step[h](1)),
                send(pb.at[h, 1, ps, pl.ds(64, 64)], ra.at[h, 1, ps], step[h](-1)),
            )

    def send_b(g):
        lo, hi = GROUPS[g]
        ps = pl.ds(lo, hi - lo)
        for h in range(2):
            s_b[h, g] = (
                send(pb.at[h, 0, ps, pl.ds(64, 64)], rx.at[h, 0, ps, pl.ds(64, 64)], step[h](1)),
                send(pb.at[h, 2, ps, pl.ds(0, 64)], rx.at[h, 1, ps, pl.ds(0, 64)], step[h](-1)),
            )

    def send_c(g):
        lo, hi = GROUPS[g]
        ps = pl.ds(lo, hi - lo)
        for h in range(2):
            pair = []
            for s in range(2):
                s_a[h, g][s].wait_recv()
                for p in range(lo, hi):
                    cb[h, s, p] = (pc[h, s, p] + ra[h, s, p].astype(F32)).astype(BF16)
                pair.append(
                    send(cb.at[h, s, ps], rx.at[h, s, ps, pl.ds(64 * s, 64)], step[h](1 - 2 * s))
                )
            s_c[h, g] = pair

    def gathered(g):
        lo, hi = GROUPS[g]
        for h in range(2):
            for s in range(2):
                s_b[h, g][s].wait_recv()
                s_c[h, g][s].wait_recv()
            for p in range(lo, hi):
                ss[h, p] = pf[h, p] + rx[h, 0, p].astype(F32) + rx[h, 1, p].astype(F32)

    product(((2, 2), (2, 1)))
    product(((2, 3), (1, 2)))
    send_a(0)
    product(((3, 2), (1, 1)))
    send_b(0)
    send_a(1)
    product(((1, 3), (3, 1)))
    product(((3, 3), (0, 2)))
    send_b(1)
    product(((2, 0), (0, 1)))
    send_a(2)
    product(((0, 3), (1, 0)))
    product(((3, 0), (0, 0)))
    send_b(2)
    send_c(0)

    send_c(1)
    gathered(0)
    p2a = [
        (
            send(ss.at[h, 0, pl.ds(0, 64)], ra2.at[h, 0], step[1 - h](1)),
            send(ss.at[h, 0, pl.ds(64, 64)], ra2.at[h, 1], step[1 - h](-1)),
        )
        for h in range(2)
    ]
    send_c(2)

    def act_rows(dy):
        share_w[dy].wait_recv()
        for dx in (0, 2):
            w = wr[dy, dx : dx + 2].reshape(256, KV)
            out = lax.dot_general(kg[...], w, NT, preferred_element_type=F32).astype(BF16)
            act_v[:, columns(dy, dx)] = out[:, :128]
            act_v[:, columns(dy, dx + 1)] = out[:, 128:]

    act_rows(0)
    act_rows(1)

    gathered(1)
    p2b = [
        (
            send(ss.at[h, 1, pl.ds(64, 64)], rx2.at[h, 0, pl.ds(64, 64)], step[1 - h](1)),
            send(ss.at[h, 2, pl.ds(0, 64)], rx2.at[h, 1, pl.ds(0, 64)], step[1 - h](-1)),
        )
        for h in range(2)
    ]
    p2c = []
    for h in range(2):
        for s in range(2):
            p2a[h][s].wait_recv()
            cb2[h, s] = ss[h, 1 + s, 64 * s : 64 * s + 64] + ra2[h, s]
            p2c.append(send(cb2.at[h, s], rx2.at[h, s, pl.ds(64 * s, 64)], step[1 - h](1 - 2 * s)))

    act_rows(2)
    act_rows(3)
    store = pltpu.make_async_copy(act_v, act_out, lsem.at[4])
    store.start()

    gathered(2)
    for h in range(2):
        for s in range(2):
            p2b[h][s].wait_recv()
            p2c[2 * h + s].wait_recv()
        tb[:, 128 * h : 128 * h + 128] = (ss[h, 3] + rx2[h, 0] + rx2[h, 1]).T
    swap = send(tb.at[pl.ds(pl.multiple_of(64 * (1 - core), 64), 64)], wsw, dev(dc=1))
    wg_out[:, pl.ds(own, 256)] = tb[pl.ds(pl.multiple_of(64 * core, 64), 64)]
    swap.wait_recv()
    wg_out[:, pl.ds(pl.multiple_of(256 * (1 - core), 256), 256)] = wsw[...]
    store.wait()
    assert len(started) == N_SEMS
    for c in started:
        c.wait_send()


def shards(acts, key_grads, key_weight, lengths, threshold):
    hbm = pl.BlockSpec(memory_space=pltpu.HBM)
    anywhere = pl.BlockSpec(memory_space=pl.ANY)
    smem = pl.BlockSpec(memory_space=pltpu.SMEM)
    v = pltpu.VMEM
    act_part, weight_part = pl.pallas_call(
        kernel,
        out_shape=(
            jax.ShapeDtypeStruct((TOK, D), BF16),
            jax.ShapeDtypeStruct((D // 32, KV), F32),
        ),
        in_specs=[hbm, hbm, hbm, smem, smem],
        out_specs=(anywhere, pl.BlockSpec(memory_space=v)),
        scratch_shapes=[
            v((2, TOK, D), BF16),
            v((TOK, KV), BF16),
            v((TOK, 256), BF16),
            v((256, 2 * TOK), BF16),
            v((256, 2 * TOK), BF16),
            v((4, 4, 2, 64, KV), BF16),
            v((TOK, D), BF16),
            v((1, TOK), F32),
            v((8, 1, TOK), F32),
            v((2, 1, TOK), F32),
            v((2, 2, 1, TOK), F32),
            v((1, TOK), F32),
            v((1, TOK), F32),
            v((2, 3, 4, 128, 128), BF16),
            v((2, 2, 4, 64, 128), F32),
            v((2, 4, 128, 128), F32),
            v((2, 2, 4, 64, 128), BF16),
            v((2, 2, 4, 64, 128), BF16),
            v((2, 2, 4, 128, 128), BF16),
            v((2, 4, 128, 128), F32),
            v((2, 2, 64, 128), F32),
            v((2, 2, 64, 128), F32),
            v((2, 2, 128, 128), F32),
            v((128, 256), F32),
            v((64, 256), F32),
            pltpu.SemaphoreType.DMA((N_SEMS,)),
            pltpu.SemaphoreType.DMA((N_SEMS,)),
            pltpu.SemaphoreType.DMA((5,)),
        ],
        compiler_params=pltpu.CompilerParams(
            collective_id=0, has_side_effects=True, vmem_limit_bytes=48 * 2**20
        ),
    )(acts[0], key_grads[0], key_weight[0], lengths, threshold.reshape(1, 1))
    return (act_part[None], weight_part[None])


def solution(mesh):
    in_specs = (
        P("section", "dp", None),
        P("section", "dp", None),
        P("section", "dp", None),
        P("dp", None),
        P(),
    )
    out_specs = (P("section", "dp", None), P("section", "dp", None))
    return jax.shard_map(shards, mesh=mesh, in_specs=in_specs, out_specs=out_specs, check_vma=False)
```

```python
import jax
import jax.numpy as jnp
from jax import lax
from jax.experimental import pallas as pl
from jax.experimental.pallas import tpu as pltpu
from jax.sharding import PartitionSpec as P

MESH = pl.DeviceIdType.MESH
F32, BF16 = jnp.float32, jnp.bfloat16
NT = (((1,), (1,)), ((), ()))
D, KV, TOK, PAT = 2048, 512, 512, 16
POS = {2: 0, 1: 1, 3: 2, 0: 3}
GROUPS = ((0, 1), (1, 3), (3, 4))
N_SEMS = 109
VMEM = 58000 * 1024


def kernel(
    acts_hbm, kg_hbm, w_hbm, len_ref, thr_ref, act_out, wg_out,
    acts, kg, kgs, kgt, sct, wr, act_v,
    zv, zr, z2s, z2r, z9s, z9r,
    pb, pc, pf, ra, cb, rx, ss, ra2, cb2, rx2, wsw,
    ssem, rsem, wsem, lsem,
):
    z = lax.axis_index("section")
    dp = lax.axis_index("dp")
    core = lax.rem(dp, 2)
    xx = lax.rem(lax.div(dp, 2), 4)
    yy = lax.div(dp, 8)

    def dev(dy=0, dx=0, dc=0, dz=0, at_core=None):
        y2, x2 = lax.rem(yy + dy + 4, 4), lax.rem(xx + dx + 4, 4)
        c2 = 1 - core if dc else core
        if at_core is not None:
            c2 = at_core
        return (lax.rem(z + dz + 16, 16), (y2 * 4 + x2) * 2 + c2)

    started = []

    def send(src, dst, to, arrival=None):
        k = len(started)
        copy = pltpu.make_async_remote_copy(
            src_ref=src, dst_ref=dst, send_sem=ssem.at[k],
            recv_sem=rsem.at[k] if arrival is None else arrival, device_id=to, device_id_type=MESH,
        )
        copy.start()
        started.append(copy)
        return copy

    load_kg = pltpu.make_async_copy(kg_hbm, kg, lsem.at[0])
    load_lo = pltpu.make_async_copy(acts_hbm.at[0:256], acts.at[0, 0:256], lsem.at[1])
    load_hi = pltpu.make_async_copy(acts_hbm.at[256:512], acts.at[0, 256:512], lsem.at[2])
    load_w = pltpu.make_async_copy(w_hbm, wr.at[0, 0, core], lsem.at[3])
    load_kg.start()
    load_lo.start()
    load_hi.start()
    load_w.start()

    near = [dev(dc=1), dev(dx=1), dev(dx=-1), dev(dy=1), dev(dy=-1)]
    zs = [1, -1, 2, -2, 3, -3, 4, -4]
    partners = near + [dev(dz=k) for k in zs] + [dev(dz=4, dc=1), dev(dz=-4, dc=1)]
    barrier = pltpu.get_barrier_semaphore()
    for who in partners:
        pl.semaphore_signal(barrier, inc=1, device_id=who, device_id_type=MESH)

    lane = lax.broadcasted_iota(jnp.int32, (1, TOK), 1)
    sub = lax.broadcasted_iota(jnp.int32, (TOK, 1), 0)
    seg_row = jnp.zeros((1, TOK), jnp.int32)
    seg_col = jnp.zeros((TOK, 1), jnp.int32)
    end = jnp.int32(0)
    for p in range(PAT):
        end = end + len_ref[0, p]
        seg_row = seg_row + (lane >= end).astype(jnp.int32)
        seg_col = seg_col + (sub >= end).astype(jnp.int32)


    def masked(rows, cols):
        (r0, r1), (c0, c1) = rows, cols
        gx = lax.dot_general(acts[0, r0:r1], acts[0, c0:c1], NT, preferred_element_type=F32)
        gg = lax.dot_general(kg[r0:r1], kg[c0:c1], NT, preferred_element_type=F32)
        same = seg_col[r0:r1] == seg_row[:, c0:c1]
        return same, jnp.sum(jnp.where(same, gx * gg, 0.0), axis=1, keepdims=True)

    def spread(same, r):
        return jnp.sum(jnp.where(same, r, 0.0), axis=0, keepdims=True)

    load_kg.wait()
    load_lo.wait()
    same_a, r_a = masked((0, 256), (0, 256))
    load_hi.wait()
    same_c, r_c = masked((128, 256), (256, 384))
    same_b, r_b = masked((256, 512), (256, 512))
    r_1 = r_a[128:] + 2.0 * r_c
    same_t = seg_col[256:384] == seg_row[:, 128:256]
    v_a = spread(same_a[:128], r_a[:128]) + spread(same_a[128:], r_1)
    v_b = spread(same_b, r_b)
    zv[:, 0:128] = v_a[:, 0:128]
    zv[:, 128:256] = v_a[:, 128:256] + spread(same_t, r_b[:128])
    zv[:, 256:384] = v_b[:, 0:128] + spread(same_c, r_1)
    zv[:, 384:512] = v_b[:, 128:256]

    pl.semaphore_wait(barrier, len(partners))
    z1 = [send(zv, zr.at[i], dev(dz=k)) for i, k in enumerate(zs)]

    step = (lambda s, c=None: dev(dx=s, at_core=c), lambda s, c=None: dev(dy=s, at_core=c))

    def at(h, d1, d2):
        return (d2, d1) if h == 0 else (d1, d2)

    def slot(h, d1, d2, lo=0, hi=32):
        return wr.at[(*at(h, d1, d2), core, pl.ds(32 * h + lo, hi - lo))]

    g_a1, g_a2, g_b1, g_b2 = {}, {}, {}, {}
    for h in range(2):
        mine = w_hbm.at[pl.ds(32 * h, 32)]
        g_a1[h] = (
            send(mine, slot(h, 3, 0), step[h](1)),
            send(mine, slot(h, 1, 0), step[h](-1)),
        )

    def second(h, d1):
        mine = slot(h, d1, 0) if d1 else w_hbm.at[pl.ds(32 * h, 32)]
        return (
            send(mine, slot(h, d1, 3), step[1 - h](1)),
            send(mine, slot(h, d1, 1), step[1 - h](-1)),
        )

    def second_forward(h, d1):
        for c in g_b1[h, d1]:
            c.wait_recv()
        g_b2[h, d1] = (
            send(slot(h, d1, 3, 0, 16), slot(h, d1, 2, 0, 16), step[1 - h](1)),
            send(slot(h, d1, 1, 16, 32), slot(h, d1, 2, 16, 32), step[1 - h](-1)),
        )

    for h in range(2):
        g_b1[h, 0] = second(h, 0)
    share_kg = send(
        kg_hbm.at[:, pl.ds(pl.multiple_of(256 * (1 - core), 256), 256)], kgs, dev(dc=1)
    )
    share_acts = send(acts_hbm, acts.at[1], dev(dc=1))


    own = pl.multiple_of(256 * core, 256)
    kgt[:, 0:512] = kg[:, pl.ds(own, 256)].T

    for h in range(2):
        for c in g_a1[h]:
            c.wait_recv()
        g_a2[h] = (
            send(slot(h, 3, 0, 0, 16), slot(h, 2, 0, 0, 16), step[h](1)),
            send(slot(h, 1, 0, 16, 32), slot(h, 2, 0, 16, 32), step[h](-1)),
        )
    for h in range(2):
        for d1 in (1, 3):
            g_b1[h, d1] = second(h, d1)
    for h in range(2):
        for c in g_a2[h]:
            c.wait_recv()
        g_b1[h, 2] = second(h, 2)
        second_forward(h, 0)

    share_kg.wait_recv()
    kgt[:, 512:1024] = kgs[...].T

    for c in z1[0::2]:
        c.wait_recv()
    up = zr[0] + zr[2] + zr[4] + zr[6]
    z2s[0] = up
    z2 = [
        send(z2s.at[0], z2r.at[0, 0], dev(dz=4)),
        send(z2s.at[0], z2r.at[1, 0], dev(dz=4, dc=1)),
    ]
    for c in z1[1::2]:
        c.wait_recv()
    down = zr[1] + zr[3] + zr[5]
    z2s[1] = down
    z2 += [
        send(z2s.at[1], z2r.at[0, 1], dev(dz=-4)),
        send(z2s.at[1], z2r.at[1, 1], dev(dz=-4, dc=1)),
    ]
    nine = zv[...] + up + (down + zr[7])
    z9s[...] = nine
    z2.append(send(z9s, z9r, dev(dc=1)))

    for d1 in (1, 3):
        for h in range(2):
            second_forward(h, d1)
    for h in range(2):
        second_forward(h, 2)

    load_w.wait()
    for h in range(2):
        for d1 in range(4):
            for c in g_b2[h, d1]:
                c.wait_recv()
    share_w = [
        send(wr.at[dy, :, core], wr.at[dy, :, core], dev(dc=1)) for dy in range(4)
    ]

    for c in z2:
        c.wait_recv()
    thr = thr_ref[0, 0]
    for s, total in ((0, nine + (z2r[0, 0] + z2r[0, 1])), (1, z9r[...] + (z2r[1, 0] + z2r[1, 1]))):
        factor = thr / jnp.maximum(jnp.sqrt(total), thr)
        cols = slice(512 * s, 512 * s + 512)
        sct[:, cols] = (kgt[:, cols].astype(F32) * factor).astype(BF16)
    share_acts.wait_recv()

    def chip(dy, dx):
        return lax.rem(yy + dy, 4) * 4 + lax.rem(xx + dx, 4)

    def columns(dy, dx):
        return pl.ds(pl.multiple_of(128 * chip(dy, dx), 128), 128)

    def product(pair):
        out = None
        for s in range(2):
            rhs = jnp.concatenate([acts[s, :, columns(*q)] for q in pair], axis=1)
            part = jnp.dot(sct[:, 512 * s : 512 * s + 512], rhs, preferred_element_type=F32)
            out = part if out is None else out + part
        for i, (dy, dx) in enumerate(pair):
            for h in range(2):
                d1, d2 = (dx, dy) if h == 0 else (dy, dx)
                r = out[128 * h : 128 * h + 128, 128 * i : 128 * i + 128]
                p = POS[d2]
                if d1 == 0:
                    pf[h, p] = r
                elif d1 == 2:
                    pb[h, 1, p] = r.astype(BF16)
                elif d1 == 1:
                    pc[h, 0, p] = r[:64]
                    pb[h, 0, p, 64:] = r[64:].astype(BF16)
                else:
                    pb[h, 2, p, :64] = r[:64].astype(BF16)
                    pc[h, 1, p] = r[64:]

    s_a, s_b, s_c = {}, {}, {}

    def send_a(g):
        lo, hi = GROUPS[g]
        ps = pl.ds(lo, hi - lo)
        for h in range(2):
            s_a[h, g] = (
                send(pb.at[h, 1, ps, pl.ds(0, 64)], ra.at[h, 0, ps], step[h](1)),
                send(pb.at[h, 1, ps, pl.ds(64, 64)], ra.at[h, 1, ps], step[h](-1)),
            )

    def send_b(g):
        lo, hi = GROUPS[g]
        ps = pl.ds(lo, hi - lo)
        for h in range(2):
            s_b[h, g] = (
                send(pb.at[h, 0, ps, pl.ds(64, 64)], rx.at[h, 0, ps, pl.ds(64, 64)], step[h](1)),
                send(pb.at[h, 2, ps, pl.ds(0, 64)], rx.at[h, 1, ps, pl.ds(0, 64)], step[h](-1)),
            )

    def send_c(g):
        lo, hi = GROUPS[g]
        ps = pl.ds(lo, hi - lo)
        for h in range(2):
            pair = []
            for s in range(2):
                s_a[h, g][s].wait_recv()
                for p in range(lo, hi):
                    cb[h, s, p] = (pc[h, s, p] + ra[h, s, p].astype(F32)).astype(BF16)
                pair.append(
                    send(cb.at[h, s, ps], rx.at[h, s, ps, pl.ds(64 * s, 64)], step[h](1 - 2 * s))
                )
            s_c[h, g] = pair

    def gathered(g):
        lo, hi = GROUPS[g]
        for h in range(2):
            for s in range(2):
                s_b[h, g][s].wait_recv()
                s_c[h, g][s].wait_recv()
            for p in range(lo, hi):
                ss[h, p] = (pf[h, p] + rx[h, 0, p].astype(F32) + rx[h, 1, p].astype(F32)).T

    product(((2, 2), (2, 1)))
    product(((2, 3), (1, 2)))
    send_a(0)
    product(((3, 2), (1, 1)))
    send_b(0)
    send_a(1)
    product(((1, 3), (3, 1)))
    product(((3, 3), (0, 2)))
    send_b(1)
    product(((2, 0), (0, 1)))
    send_a(2)
    product(((0, 3), (1, 0)))
    product(((3, 0), (0, 0)))
    send_b(2)
    send_c(0)

    send_c(1)
    gathered(0)
    p2a = [
        (
            send(ss.at[h, 0, pl.ds(0, 64)], ra2.at[h, 0], step[1 - h](1)),
            send(ss.at[h, 0, pl.ds(64, 64)], ra2.at[h, 1], step[1 - h](-1)),
        )
        for h in range(2)
    ]
    send_c(2)

    def act_rows(dy):
        share_w[dy].wait_recv()
        for dx in (0, 2):
            w = wr[dy, dx : dx + 2].reshape(256, KV)
            out = lax.dot_general(kg[...], w, NT, preferred_element_type=F32).astype(BF16)
            act_v[:, columns(dy, dx)] = out[:, :128]
            act_v[:, columns(dy, dx + 1)] = out[:, 128:]

    act_rows(0)
    act_rows(1)

    gathered(1)
    def last(src, h, s, c):
        return send(src, rx2.at[core, h, s], step[1 - h](1 - 2 * s, c), wsem.at[core, h, s])

    for h in range(2):
        last(ss.at[h, 1, pl.ds(64, 64)], h, 0, 1)
        last(ss.at[h, 2, pl.ds(0, 64)], h, 1, 0)
    for h in range(2):
        for s in range(2):
            p2a[h][s].wait_recv()
            cb2[h, s] = ss[h, 1 + s, 64 * s : 64 * s + 64] + ra2[h, s]
            last(cb2.at[h, s], h, s, s)

    act_rows(2)
    act_rows(3)
    store = pltpu.make_async_copy(act_v, act_out, lsem.at[4])
    store.start()

    gathered(2)
    given = [
        send(ss.at[h, 3, pl.ds(pl.multiple_of(64 * (1 - core), 64), 64)], wsw.at[h], dev(dc=1))
        for h in range(2)
    ]
    for h in range(2):
        given[h].wait_recv()
    for c in range(2):
        for h in range(2):
            for s in range(2):
                pltpu.make_async_remote_copy(
                    src_ref=cb2.at[h, s], dst_ref=rx2.at[c, h, s], send_sem=ssem.at[0],
                    recv_sem=wsem.at[c, h, s], device_id=dev(dc=1), device_id_type=MESH,
                ).wait_recv()
    mine = pl.ds(pl.multiple_of(64 * core, 64), 64)
    for h in range(2):
        near = pl.ds(pl.multiple_of(256 * core + 128 * h, 128), 128)
        far = pl.ds(pl.multiple_of(256 * (1 - core) + 128 * h, 128), 128)
        wg_out[:, near] = ss[h, 3, mine] + rx2[core, h, 0] + rx2[core, h, 1]
        wg_out[:, far] = wsw[h] + rx2[1 - core, h, 0] + rx2[1 - core, h, 1]
    store.wait()
    assert len(started) == N_SEMS
    for c in started:
        c.wait_send()


def finish(act_in, wg_in, act_out, wg_out, act_v, wg_v, sems):
    parts = [(wg_in, wg_v, wg_out)]
    for k in range(8):
        rows = pl.ds(64 * k, 64)
        parts.append((act_in.at[rows], act_v.at[rows], act_out.at[rows]))
    loads = [pltpu.make_async_copy(a, b, sems.at[0, k]) for k, (a, b, _) in enumerate(parts)]
    stores = [pltpu.make_async_copy(b, c, sems.at[1, k]) for k, (_, b, c) in enumerate(parts)]
    for c in loads:
        c.start()
    for c, d in zip(loads, stores):
        c.wait()
        d.start()
    for d in stores:
        d.wait()


def shards(acts, key_grads, key_weight, lengths, threshold):
    hbm = pl.BlockSpec(memory_space=pltpu.HBM)
    anywhere = pl.BlockSpec(memory_space=pl.ANY)
    smem = pl.BlockSpec(memory_space=pltpu.SMEM)
    v = pltpu.VMEM
    act_part, weight_part = pl.pallas_call(
        kernel,
        out_shape=(
            jax.ShapeDtypeStruct((TOK, D), BF16),
            jax.ShapeDtypeStruct((D // 32, KV), F32),
        ),
        in_specs=[hbm, hbm, hbm, smem, smem],
        out_specs=(anywhere, pl.BlockSpec(memory_space=v)),
        scratch_shapes=[
            v((2, TOK, D), BF16),
            v((TOK, KV), BF16),
            v((TOK, 256), BF16),
            v((256, 2 * TOK), BF16),
            v((256, 2 * TOK), BF16),
            v((4, 4, 2, 64, KV), BF16),
            v((TOK, D), BF16),
            v((1, TOK), F32),
            v((8, 1, TOK), F32),
            v((2, 1, TOK), F32),
            v((2, 2, 1, TOK), F32),
            v((1, TOK), F32),
            v((1, TOK), F32),
            v((2, 3, 4, 128, 128), BF16),
            v((2, 2, 4, 64, 128), F32),
            v((2, 4, 128, 128), F32),
            v((2, 2, 4, 64, 128), BF16),
            v((2, 2, 4, 64, 128), BF16),
            v((2, 2, 4, 128, 128), BF16),
            v((2, 4, 128, 128), F32),
            v((2, 2, 64, 128), F32),
            v((2, 2, 64, 128), F32),
            v((2, 2, 2, 64, 128), F32),
            v((2, 64, 128), F32),
            pltpu.SemaphoreType.DMA((N_SEMS,)),
            pltpu.SemaphoreType.DMA((N_SEMS,)),
            pltpu.SemaphoreType.DMA((2, 2, 2)),
            pltpu.SemaphoreType.DMA((5,)),
        ],
        compiler_params=pltpu.CompilerParams(
            collective_id=0, has_side_effects=True, vmem_limit_bytes=VMEM
        ),
    )(acts[0], key_grads[0], key_weight[0], lengths, threshold.reshape(1, 1))
    act_part, weight_part = pl.pallas_call(
        finish,
        out_shape=(
            jax.ShapeDtypeStruct((TOK, D), BF16),
            jax.ShapeDtypeStruct((D // 32, KV), F32),
        ),
        in_specs=[hbm, hbm],
        out_specs=(hbm, hbm),
        scratch_shapes=[v((TOK, D), BF16), v((D // 32, KV), F32), pltpu.SemaphoreType.DMA((2, 9))],
        compiler_params=pltpu.CompilerParams(vmem_limit_bytes=VMEM),
    )(act_part, weight_part)
    return (act_part[None], weight_part[None])


def solution(mesh):
    in_specs = (
        P("section", "dp", None),
        P("section", "dp", None),
        P("section", "dp", None),
        P("dp", None),
        P(),
    )
    out_specs = (P("section", "dp", None), P("section", "dp", None))
    return jax.shard_map(shards, mesh=mesh, in_specs=in_specs, out_specs=out_specs, check_vma=False)
```

```python
import jax
import jax.numpy as jnp
from jax import lax
from jax.experimental import pallas as pl
from jax.experimental.pallas import tpu as pltpu
from jax.sharding import PartitionSpec as P

MESH = pl.DeviceIdType.MESH
F32, BF16 = jnp.float32, jnp.bfloat16
NT = (((1,), (1,)), ((), ()))
D, KV, TOK, PAT = 2048, 512, 512, 16
POS = {2: 0, 1: 1, 3: 2, 0: 3}
GROUPS = ((0, 1), (1, 3), (3, 4))
N_SEMS = 112
VMEM = 58000 * 1024


def kernel(
    acts_hbm, kg_hbm, w_hbm, len_ref, thr_ref, act_out, wg_out,
    acts, kg, kgs, kgt, sct, wr, act_v,
    zv, zr, z9s, z9r,
    pb, pc, pf, ra, cb, rx, ss, ra2, cb2, rx2, wsw,
    ssem, rsem, wsem, lsem,
):
    z = lax.axis_index("section")
    dp = lax.axis_index("dp")
    core = lax.rem(dp, 2)
    xx = lax.rem(lax.div(dp, 2), 4)
    yy = lax.div(dp, 8)

    def dev(dy=0, dx=0, dc=0, dz=0, at_core=None):
        y2, x2 = lax.rem(yy + dy + 4, 4), lax.rem(xx + dx + 4, 4)
        c2 = 1 - core if dc else core
        if at_core is not None:
            c2 = at_core
        return (lax.rem(z + dz + 16, 16), (y2 * 4 + x2) * 2 + c2)

    started = []

    def send(src, dst, to, arrival=None):
        k = len(started)
        copy = pltpu.make_async_remote_copy(
            src_ref=src, dst_ref=dst, send_sem=ssem.at[k],
            recv_sem=rsem.at[k] if arrival is None else arrival, device_id=to, device_id_type=MESH,
        )
        copy.start()
        started.append(copy)
        return copy

    load_kg = pltpu.make_async_copy(kg_hbm, kg, lsem.at[0])
    load_lo = pltpu.make_async_copy(acts_hbm.at[0:256], acts.at[0, 0:256], lsem.at[1])
    load_hi = pltpu.make_async_copy(acts_hbm.at[256:512], acts.at[0, 256:512], lsem.at[2])
    load_w = pltpu.make_async_copy(w_hbm, wr.at[0, 0, core], lsem.at[3])
    load_kg.start()
    load_lo.start()
    load_hi.start()
    load_w.start()

    near = [dev(dc=1), dev(dx=1), dev(dx=-1), dev(dy=1), dev(dy=-1)]
    zs = [8] + [s * k for k in range(7, 0, -1) for s in (1, -1)]
    partners = near + [dev(dz=k) for k in zs]
    barrier = pltpu.get_barrier_semaphore()
    for who in partners:
        pl.semaphore_signal(barrier, inc=1, device_id=who, device_id_type=MESH)

    lane = lax.broadcasted_iota(jnp.int32, (1, TOK), 1)
    sub = lax.broadcasted_iota(jnp.int32, (TOK, 1), 0)
    seg_row = jnp.zeros((1, TOK), jnp.int32)
    seg_col = jnp.zeros((TOK, 1), jnp.int32)
    end = jnp.int32(0)
    for p in range(PAT):
        end = end + len_ref[0, p]
        seg_row = seg_row + (lane >= end).astype(jnp.int32)
        seg_col = seg_col + (sub >= end).astype(jnp.int32)


    def masked(rows, cols):
        (r0, r1), (c0, c1) = rows, cols
        gx = lax.dot_general(acts[0, r0:r1], acts[0, c0:c1], NT, preferred_element_type=F32)
        gg = lax.dot_general(kg[r0:r1], kg[c0:c1], NT, preferred_element_type=F32)
        same = seg_col[r0:r1] == seg_row[:, c0:c1]
        return same, jnp.sum(jnp.where(same, gx * gg, 0.0), axis=1, keepdims=True)

    def spread(same, r):
        return jnp.sum(jnp.where(same, r, 0.0), axis=0, keepdims=True)

    load_kg.wait()
    load_lo.wait()
    same_a, r_a = masked((0, 256), (0, 256))
    load_hi.wait()
    same_c, r_c = masked((128, 256), (256, 384))
    same_b, r_b = masked((256, 512), (256, 512))
    r_1 = r_a[128:] + 2.0 * r_c
    same_t = seg_col[256:384] == seg_row[:, 128:256]
    v_a = spread(same_a[:128], r_a[:128]) + spread(same_a[128:], r_1)
    v_b = spread(same_b, r_b)
    zv[:, 0:128] = v_a[:, 0:128]
    zv[:, 128:256] = v_a[:, 128:256] + spread(same_t, r_b[:128])
    zv[:, 256:384] = v_b[:, 0:128] + spread(same_c, r_1)
    zv[:, 384:512] = v_b[:, 128:256]

    pl.semaphore_wait(barrier, len(partners))
    z1 = [send(zv, zr.at[i], dev(dz=k)) for i, k in enumerate(zs)]

    step = (lambda s, c=None: dev(dx=s, at_core=c), lambda s, c=None: dev(dy=s, at_core=c))

    def at(h, d1, d2):
        return (d2, d1) if h == 0 else (d1, d2)

    def slot(h, d1, d2, lo=0, hi=32):
        return wr.at[(*at(h, d1, d2), core, pl.ds(32 * h + lo, hi - lo))]

    g_a1, g_a2, g_b1, g_b2 = {}, {}, {}, {}
    for h in range(2):
        mine = w_hbm.at[pl.ds(32 * h, 32)]
        g_a1[h] = (
            send(mine, slot(h, 3, 0), step[h](1)),
            send(mine, slot(h, 1, 0), step[h](-1)),
        )

    def second(h, d1):
        mine = slot(h, d1, 0) if d1 else w_hbm.at[pl.ds(32 * h, 32)]
        return (
            send(mine, slot(h, d1, 3), step[1 - h](1)),
            send(mine, slot(h, d1, 1), step[1 - h](-1)),
        )

    def second_forward(h, d1):
        for c in g_b1[h, d1]:
            c.wait_recv()
        g_b2[h, d1] = (
            send(slot(h, d1, 3, 0, 16), slot(h, d1, 2, 0, 16), step[1 - h](1)),
            send(slot(h, d1, 1, 16, 32), slot(h, d1, 2, 16, 32), step[1 - h](-1)),
        )

    for h in range(2):
        g_b1[h, 0] = second(h, 0)
    share_kg = send(
        kg_hbm.at[:, pl.ds(pl.multiple_of(256 * (1 - core), 256), 256)], kgs, dev(dc=1)
    )
    share_acts = send(acts_hbm, acts.at[1], dev(dc=1))


    own = pl.multiple_of(256 * core, 256)
    kgt[:, 0:512] = kg[:, pl.ds(own, 256)].T

    for h in range(2):
        for c in g_a1[h]:
            c.wait_recv()
        g_a2[h] = (
            send(slot(h, 3, 0, 0, 16), slot(h, 2, 0, 0, 16), step[h](1)),
            send(slot(h, 1, 0, 16, 32), slot(h, 2, 0, 16, 32), step[h](-1)),
        )
    for h in range(2):
        for d1 in (1, 3):
            g_b1[h, d1] = second(h, d1)
    for h in range(2):
        for c in g_a2[h]:
            c.wait_recv()
        g_b1[h, 2] = second(h, 2)
        second_forward(h, 0)

    share_kg.wait_recv()
    kgt[:, 512:1024] = kgs[...].T


    for c in z1:
        c.wait_recv()
    both = zv[...]
    for i in range(15):
        both = both + zr[i]
    z9s[...] = both
    give = send(z9s, z9r, dev(dc=1))
    thr = thr_ref[0, 0]
    for s in range(2):
        if s == 1:
            give.wait_recv()
        total = z9r[...] if s else both
        factor = thr / jnp.maximum(jnp.sqrt(total), thr)
        cols = slice(512 * s, 512 * s + 512)
        sct[:, cols] = (kgt[:, cols].astype(F32) * factor).astype(BF16)
    share_acts.wait_recv()

    def chip(dy, dx):
        return lax.rem(yy + dy, 4) * 4 + lax.rem(xx + dx, 4)

    def columns(dy, dx):
        return pl.ds(pl.multiple_of(128 * chip(dy, dx), 128), 128)

    def product(pair):
        out = None
        for s in range(2):
            rhs = jnp.concatenate([acts[s, :, columns(*q)] for q in pair], axis=1)
            part = jnp.dot(sct[:, 512 * s : 512 * s + 512], rhs, preferred_element_type=F32)
            out = part if out is None else out + part
        for i, (dy, dx) in enumerate(pair):
            for h in range(2):
                d1, d2 = (dx, dy) if h == 0 else (dy, dx)
                r = out[128 * h : 128 * h + 128, 128 * i : 128 * i + 128]
                p = POS[d2]
                if d1 == 0:
                    pf[h, p] = r
                elif d1 == 2:
                    pb[h, 1, p] = r.astype(BF16)
                elif d1 == 1:
                    pc[h, 0, p] = r[:64]
                    pb[h, 0, p, 64:] = r[64:].astype(BF16)
                else:
                    pb[h, 2, p, :64] = r[:64].astype(BF16)
                    pc[h, 1, p] = r[64:]

    s_a, s_b, s_c = {}, {}, {}

    def send_a(g):
        lo, hi = GROUPS[g]
        ps = pl.ds(lo, hi - lo)
        for h in range(2):
            s_a[h, g] = (
                send(pb.at[h, 1, ps, pl.ds(0, 64)], ra.at[h, 0, ps], step[h](1)),
                send(pb.at[h, 1, ps, pl.ds(64, 64)], ra.at[h, 1, ps], step[h](-1)),
            )

    def send_b(g):
        lo, hi = GROUPS[g]
        ps = pl.ds(lo, hi - lo)
        for h in range(2):
            s_b[h, g] = (
                send(pb.at[h, 0, ps, pl.ds(64, 64)], rx.at[h, 0, ps, pl.ds(64, 64)], step[h](1)),
                send(pb.at[h, 2, ps, pl.ds(0, 64)], rx.at[h, 1, ps, pl.ds(0, 64)], step[h](-1)),
            )

    def send_c(g):
        lo, hi = GROUPS[g]
        ps = pl.ds(lo, hi - lo)
        for h in range(2):
            pair = []
            for s in range(2):
                s_a[h, g][s].wait_recv()
                for p in range(lo, hi):
                    cb[h, s, p] = (pc[h, s, p] + ra[h, s, p].astype(F32)).astype(BF16)
                pair.append(
                    send(cb.at[h, s, ps], rx.at[h, s, ps, pl.ds(64 * s, 64)], step[h](1 - 2 * s))
                )
            s_c[h, g] = pair

    def gathered(g):
        lo, hi = GROUPS[g]
        for h in range(2):
            for s in range(2):
                s_b[h, g][s].wait_recv()
                s_c[h, g][s].wait_recv()
            for p in range(lo, hi):
                ss[h, p] = (pf[h, p] + rx[h, 0, p].astype(F32) + rx[h, 1, p].astype(F32)).T

    def act_rows(dy):
        share_w[dy].wait_recv()
        for dx in (0, 2):
            w = wr[dy, dx : dx + 2].reshape(256, KV)
            out = lax.dot_general(kg[...], w, NT, preferred_element_type=F32).astype(BF16)
            act_v[:, columns(dy, dx)] = out[:, :128]
            act_v[:, columns(dy, dx + 1)] = out[:, 128:]

    product(((2, 2), (2, 1)))
    product(((2, 3), (1, 2)))
    send_a(0)
    product(((3, 2), (1, 1)))
    send_b(0)
    send_a(1)
    for d1 in (1, 3):
        for h in range(2):
            second_forward(h, d1)
    product(((1, 3), (3, 1)))
    product(((3, 3), (0, 2)))
    send_c(0)
    send_b(1)
    for h in range(2):
        second_forward(h, 2)
    product(((2, 0), (0, 1)))
    product(((0, 3), (1, 0)))
    send_a(2)
    product(((3, 0), (0, 0)))
    send_c(1)
    send_b(2)
    gathered(0)
    p2a = [
        (
            send(ss.at[h, 0, pl.ds(0, 64)], ra2.at[h, 0], step[1 - h](1)),
            send(ss.at[h, 0, pl.ds(64, 64)], ra2.at[h, 1], step[1 - h](-1)),
        )
        for h in range(2)
    ]
    load_w.wait()
    for h in range(2):
        for d1 in range(4):
            for c in g_b2[h, d1]:
                c.wait_recv()
    share_w = [
        send(wr.at[dy, :, core], wr.at[dy, :, core], dev(dc=1)) for dy in range(4)
    ]

    act_rows(0)

    gathered(1)
    def last(src, h, s, c):
        return send(src, rx2.at[core, h, s], step[1 - h](1 - 2 * s, c), wsem.at[core, h, s])

    for h in range(2):
        last(ss.at[h, 1, pl.ds(64, 64)], h, 0, 1)
        last(ss.at[h, 2, pl.ds(0, 64)], h, 1, 0)
    for h in range(2):
        for s in range(2):
            p2a[h][s].wait_recv()
            cb2[h, s] = ss[h, 1 + s, 64 * s : 64 * s + 64] + ra2[h, s]
            last(cb2.at[h, s], h, s, s)

    send_c(2)
    act_rows(1)
    act_rows(2)
    act_rows(3)
    store = pltpu.make_async_copy(act_v, act_out, lsem.at[4])
    store.start()

    gathered(2)
    given = [
        send(ss.at[h, 3, pl.ds(pl.multiple_of(64 * (1 - core), 64), 64)], wsw.at[h], dev(dc=1))
        for h in range(2)
    ]
    for h in range(2):
        given[h].wait_recv()
    for c in range(2):
        for h in range(2):
            for s in range(2):
                pltpu.make_async_remote_copy(
                    src_ref=cb2.at[h, s], dst_ref=rx2.at[c, h, s], send_sem=ssem.at[0],
                    recv_sem=wsem.at[c, h, s], device_id=dev(dc=1), device_id_type=MESH,
                ).wait_recv()
    mine = pl.ds(pl.multiple_of(64 * core, 64), 64)
    for h in range(2):
        near = pl.ds(pl.multiple_of(256 * core + 128 * h, 128), 128)
        far = pl.ds(pl.multiple_of(256 * (1 - core) + 128 * h, 128), 128)
        wg_out[:, near] = ss[h, 3, mine] + rx2[core, h, 0] + rx2[core, h, 1]
        wg_out[:, far] = wsw[h] + rx2[1 - core, h, 0] + rx2[1 - core, h, 1]
    store.wait()
    assert len(started) == N_SEMS
    for c in started:
        c.wait_send()


def finish(act_in, wg_in, act_out, wg_out, act_v, wg_v, sems):
    parts = [(wg_in, wg_v, wg_out)]
    for k in range(8):
        rows = pl.ds(64 * k, 64)
        parts.append((act_in.at[rows], act_v.at[rows], act_out.at[rows]))
    loads = [pltpu.make_async_copy(a, b, sems.at[0, k]) for k, (a, b, _) in enumerate(parts)]
    stores = [pltpu.make_async_copy(b, c, sems.at[1, k]) for k, (_, b, c) in enumerate(parts)]
    for c in loads:
        c.start()
    for c, d in zip(loads, stores):
        c.wait()
        d.start()
    for d in stores:
        d.wait()


def shards(acts, key_grads, key_weight, lengths, threshold):
    hbm = pl.BlockSpec(memory_space=pltpu.HBM)
    anywhere = pl.BlockSpec(memory_space=pl.ANY)
    smem = pl.BlockSpec(memory_space=pltpu.SMEM)
    v = pltpu.VMEM
    act_part, weight_part = pl.pallas_call(
        kernel,
        out_shape=(
            jax.ShapeDtypeStruct((TOK, D), BF16),
            jax.ShapeDtypeStruct((D // 32, KV), F32),
        ),
        in_specs=[hbm, hbm, hbm, smem, smem],
        out_specs=(anywhere, pl.BlockSpec(memory_space=v)),
        scratch_shapes=[
            v((2, TOK, D), BF16),
            v((TOK, KV), BF16),
            v((TOK, 256), BF16),
            v((256, 2 * TOK), BF16),
            v((256, 2 * TOK), BF16),
            v((4, 4, 2, 64, KV), BF16),
            v((TOK, D), BF16),
            v((1, TOK), F32),
            v((15, 1, TOK), F32),
            v((1, TOK), F32),
            v((1, TOK), F32),
            v((2, 3, 4, 128, 128), BF16),
            v((2, 2, 4, 64, 128), F32),
            v((2, 4, 128, 128), F32),
            v((2, 2, 4, 64, 128), BF16),
            v((2, 2, 4, 64, 128), BF16),
            v((2, 2, 4, 128, 128), BF16),
            v((2, 4, 128, 128), F32),
            v((2, 2, 64, 128), F32),
            v((2, 2, 64, 128), F32),
            v((2, 2, 2, 64, 128), F32),
            v((2, 64, 128), F32),
            pltpu.SemaphoreType.DMA((N_SEMS,)),
            pltpu.SemaphoreType.DMA((N_SEMS,)),
            pltpu.SemaphoreType.DMA((2, 2, 2)),
            pltpu.SemaphoreType.DMA((5,)),
        ],
        compiler_params=pltpu.CompilerParams(
            collective_id=0, has_side_effects=True, vmem_limit_bytes=VMEM
        ),
    )(acts[0], key_grads[0], key_weight[0], lengths, threshold.reshape(1, 1))
    act_part, weight_part = pl.pallas_call(
        finish,
        out_shape=(
            jax.ShapeDtypeStruct((TOK, D), BF16),
            jax.ShapeDtypeStruct((D // 32, KV), F32),
        ),
        in_specs=[hbm, hbm],
        out_specs=(hbm, hbm),
        scratch_shapes=[v((TOK, D), BF16), v((D // 32, KV), F32), pltpu.SemaphoreType.DMA((2, 9))],
        compiler_params=pltpu.CompilerParams(vmem_limit_bytes=VMEM),
    )(act_part, weight_part)
    return (act_part[None], weight_part[None])


def solution(mesh):
    in_specs = (
        P("section", "dp", None),
        P("section", "dp", None),
        P("section", "dp", None),
        P("dp", None),
        P(),
    )
    out_specs = (P("section", "dp", None), P("section", "dp", None))
    return jax.shard_map(shards, mesh=mesh, in_specs=in_specs, out_specs=out_specs, check_vma=False)
```

```python
import jax
import jax.numpy as jnp
from jax import lax
from jax.experimental import pallas as pl
from jax.experimental.pallas import tpu as pltpu
from jax.sharding import PartitionSpec as P

MESH = pl.DeviceIdType.MESH
F32, BF16 = jnp.float32, jnp.bfloat16
NT = (((1,), (1,)), ((), ()))
D, KV, TOK, PAT = 2048, 512, 512, 16
POS = {2: 0, 1: 1, 3: 2, 0: 3}
GROUPS = ((0, 1), (1, 3), (3, 4))
N_SEMS = 112
VMEM = 58000 * 1024


def kernel(
    acts_hbm, kg_hbm, w_hbm, len_ref, thr_ref, act_out, wg_out,
    acts, kg, kgs, kgt, sct, wr, act_v,
    zv, zr, z9s, z9r,
    pb, pc, pf, ra, cb, rx, ss, ra2, cb2, rx2, wsw,
    ssem, rsem, wsem, lsem,
):
    z = lax.axis_index("section")
    dp = lax.axis_index("dp")
    core = lax.rem(dp, 2)
    xx = lax.rem(lax.div(dp, 2), 4)
    yy = lax.div(dp, 8)

    def dev(dy=0, dx=0, dc=0, dz=0, at_core=None):
        y2, x2 = lax.rem(yy + dy + 4, 4), lax.rem(xx + dx + 4, 4)
        c2 = 1 - core if dc else core
        if at_core is not None:
            c2 = at_core
        return (lax.rem(z + dz + 16, 16), (y2 * 4 + x2) * 2 + c2)

    started = []

    def send(src, dst, to, arrival=None):
        k = len(started)
        copy = pltpu.make_async_remote_copy(
            src_ref=src, dst_ref=dst, send_sem=ssem.at[k],
            recv_sem=rsem.at[k] if arrival is None else arrival, device_id=to, device_id_type=MESH,
        )
        copy.start()
        started.append(copy)
        return copy

    load_kg = pltpu.make_async_copy(kg_hbm, kg, lsem.at[0])
    load_lo = pltpu.make_async_copy(acts_hbm.at[0:256], acts.at[0, 0:256], lsem.at[1])
    load_hi = pltpu.make_async_copy(acts_hbm.at[256:512], acts.at[0, 256:512], lsem.at[2])
    load_w = pltpu.make_async_copy(w_hbm, wr.at[0, 0, core], lsem.at[3])
    load_kg.start()
    load_lo.start()
    load_hi.start()
    load_w.start()

    near = [dev(dc=1), dev(dx=1), dev(dx=-1), dev(dy=1), dev(dy=-1)]
    zs = [8] + [s * k for k in range(7, 0, -1) for s in (1, -1)]
    partners = [dev(dz=k) for k in zs] + near
    barrier = pltpu.get_barrier_semaphore()
    for who in partners:
        pl.semaphore_signal(barrier, inc=1, device_id=who, device_id_type=MESH)

    lane = lax.broadcasted_iota(jnp.int32, (1, TOK), 1)
    sub = lax.broadcasted_iota(jnp.int32, (TOK, 1), 0)
    seg_row = jnp.zeros((1, TOK), jnp.int32)
    seg_col = jnp.zeros((TOK, 1), jnp.int32)
    end = jnp.int32(0)
    for p in range(PAT):
        end = end + len_ref[0, p]
        seg_row = seg_row + (lane >= end).astype(jnp.int32)
        seg_col = seg_col + (sub >= end).astype(jnp.int32)


    def masked(rows, cols):
        (r0, r1), (c0, c1) = rows, cols
        gx = lax.dot_general(acts[0, r0:r1], acts[0, c0:c1], NT, preferred_element_type=F32)
        gg = lax.dot_general(kg[r0:r1], kg[c0:c1], NT, preferred_element_type=F32)
        same = seg_col[r0:r1] == seg_row[:, c0:c1]
        return same, jnp.sum(jnp.where(same, gx * gg, 0.0), axis=1, keepdims=True)

    def spread(same, r):
        return jnp.sum(jnp.where(same, r, 0.0), axis=0, keepdims=True)

    load_kg.wait()
    load_lo.wait()
    same_a, r_a = masked((0, 256), (0, 256))
    load_hi.wait()
    same_c, r_c = masked((128, 256), (256, 384))
    same_b, r_b = masked((256, 512), (256, 512))
    r_1 = r_a[128:] + 2.0 * r_c
    same_t = seg_col[256:384] == seg_row[:, 128:256]
    v_a = spread(same_a[:128], r_a[:128]) + spread(same_a[128:], r_1)
    v_b = spread(same_b, r_b)
    zv[:, 0:128] = v_a[:, 0:128]
    zv[:, 128:256] = v_a[:, 128:256] + spread(same_t, r_b[:128])
    zv[:, 256:384] = v_b[:, 0:128] + spread(same_c, r_1)
    zv[:, 384:512] = v_b[:, 128:256]

    pl.semaphore_wait(barrier, len(partners))
    z1 = [send(zv, zr.at[i], dev(dz=k)) for i, k in enumerate(zs)]

    step = (lambda s, c=None: dev(dx=s, at_core=c), lambda s, c=None: dev(dy=s, at_core=c))

    def at(h, d1, d2):
        return (d2, d1) if h == 0 else (d1, d2)

    def slot(h, d1, d2, lo=0, hi=32):
        return wr.at[(*at(h, d1, d2), core, pl.ds(32 * h + lo, hi - lo))]

    g_a1, g_a2, g_b1, g_b2 = {}, {}, {}, {}
    for h in range(2):
        mine = w_hbm.at[pl.ds(32 * h, 32)]
        g_a1[h] = (
            send(mine, slot(h, 3, 0), step[h](1)),
            send(mine, slot(h, 1, 0), step[h](-1)),
        )

    def second(h, d1):
        mine = slot(h, d1, 0) if d1 else w_hbm.at[pl.ds(32 * h, 32)]
        return (
            send(mine, slot(h, d1, 3), step[1 - h](1)),
            send(mine, slot(h, d1, 1), step[1 - h](-1)),
        )

    def second_forward(h, d1):
        for c in g_b1[h, d1]:
            c.wait_recv()
        g_b2[h, d1] = (
            send(slot(h, d1, 3, 0, 16), slot(h, d1, 2, 0, 16), step[1 - h](1)),
            send(slot(h, d1, 1, 16, 32), slot(h, d1, 2, 16, 32), step[1 - h](-1)),
        )

    for h in range(2):
        g_b1[h, 0] = second(h, 0)
    share_kg = send(
        kg_hbm.at[:, pl.ds(pl.multiple_of(256 * (1 - core), 256), 256)], kgs, dev(dc=1)
    )
    share_acts = send(acts_hbm, acts.at[1], dev(dc=1))


    own = pl.multiple_of(256 * core, 256)
    kgt[:, 0:512] = kg[:, pl.ds(own, 256)].T

    for h in range(2):
        for c in g_a1[h]:
            c.wait_recv()
        g_a2[h] = (
            send(slot(h, 3, 0, 0, 16), slot(h, 2, 0, 0, 16), step[h](1)),
            send(slot(h, 1, 0, 16, 32), slot(h, 2, 0, 16, 32), step[h](-1)),
        )
    for h in range(2):
        for d1 in (1, 3):
            g_b1[h, d1] = second(h, d1)

    share_kg.wait_recv()
    kgt[:, 512:1024] = kgs[...].T


    for c in z1:
        c.wait_recv()
    both = zv[...]
    for i in range(15):
        both = both + zr[i]
    z9s[...] = both
    give = send(z9s, z9r, dev(dc=1))
    thr = thr_ref[0, 0]
    for s in range(2):
        if s == 1:
            give.wait_recv()
        total = z9r[...] if s else both
        factor = thr / jnp.maximum(jnp.sqrt(total), thr)
        cols = slice(512 * s, 512 * s + 512)
        sct[:, cols] = (kgt[:, cols].astype(F32) * factor).astype(BF16)
    share_acts.wait_recv()

    def chip(dy, dx):
        return lax.rem(yy + dy, 4) * 4 + lax.rem(xx + dx, 4)

    def columns(dy, dx):
        return pl.ds(pl.multiple_of(128 * chip(dy, dx), 128), 128)

    def product(pair):
        out = None
        for s in range(2):
            rhs = jnp.concatenate([acts[s, :, columns(*q)] for q in pair], axis=1)
            part = jnp.dot(sct[:, 512 * s : 512 * s + 512], rhs, preferred_element_type=F32)
            out = part if out is None else out + part
        for i, (dy, dx) in enumerate(pair):
            for h in range(2):
                d1, d2 = (dx, dy) if h == 0 else (dy, dx)
                r = out[128 * h : 128 * h + 128, 128 * i : 128 * i + 128]
                p = POS[d2]
                if d1 == 0:
                    pf[h, p] = r
                elif d1 == 2:
                    pb[h, 1, p] = r.astype(BF16)
                elif d1 == 1:
                    pc[h, 0, p] = r[:64]
                    pb[h, 0, p, 64:] = r[64:].astype(BF16)
                else:
                    pb[h, 2, p, :64] = r[:64].astype(BF16)
                    pc[h, 1, p] = r[64:]

    s_a, s_b, s_c = {}, {}, {}

    def send_a(g):
        lo, hi = GROUPS[g]
        ps = pl.ds(lo, hi - lo)
        for h in range(2):
            s_a[h, g] = (
                send(pb.at[h, 1, ps, pl.ds(0, 64)], ra.at[h, 0, ps], step[h](1)),
                send(pb.at[h, 1, ps, pl.ds(64, 64)], ra.at[h, 1, ps], step[h](-1)),
            )

    def send_b(g):
        lo, hi = GROUPS[g]
        ps = pl.ds(lo, hi - lo)
        for h in range(2):
            s_b[h, g] = (
                send(pb.at[h, 0, ps, pl.ds(64, 64)], rx.at[h, 0, ps, pl.ds(64, 64)], step[h](1)),
                send(pb.at[h, 2, ps, pl.ds(0, 64)], rx.at[h, 1, ps, pl.ds(0, 64)], step[h](-1)),
            )

    def send_c(g):
        lo, hi = GROUPS[g]
        ps = pl.ds(lo, hi - lo)
        for h in range(2):
            pair = []
            for s in range(2):
                s_a[h, g][s].wait_recv()
                for p in range(lo, hi):
                    cb[h, s, p] = (pc[h, s, p] + ra[h, s, p].astype(F32)).astype(BF16)
                pair.append(
                    send(cb.at[h, s, ps], rx.at[h, s, ps, pl.ds(64 * s, 64)], step[h](1 - 2 * s))
                )
            s_c[h, g] = pair

    def gathered(g):
        lo, hi = GROUPS[g]
        for h in range(2):
            for s in range(2):
                s_b[h, g][s].wait_recv()
                s_c[h, g][s].wait_recv()
            for p in range(lo, hi):
                ss[h, p] = (pf[h, p] + rx[h, 0, p].astype(F32) + rx[h, 1, p].astype(F32)).T

    def act_rows(dy):
        share_w[dy].wait_recv()
        for dx in (0, 2):
            w = wr[dy, dx : dx + 2].reshape(256, KV)
            out = lax.dot_general(kg[...], w, NT, preferred_element_type=F32).astype(BF16)
            act_v[:, columns(dy, dx)] = out[:, :128]
            act_v[:, columns(dy, dx + 1)] = out[:, 128:]

    product(((2, 2), (2, 1)))
    product(((2, 3), (1, 2)))
    send_a(0)
    product(((3, 2), (1, 1)))
    send_b(0)
    send_a(1)
    for h in range(2):
        for c in g_a2[h]:
            c.wait_recv()
        g_b1[h, 2] = second(h, 2)
        second_forward(h, 0)
    for d1 in (1, 3):
        for h in range(2):
            second_forward(h, d1)
    product(((1, 3), (3, 1)))
    product(((3, 3), (0, 2)))
    send_c(0)
    send_b(1)
    for h in range(2):
        second_forward(h, 2)
    product(((2, 0), (0, 1)))
    product(((0, 3), (1, 0)))
    send_a(2)
    product(((3, 0), (0, 0)))
    send_c(1)
    send_b(2)
    gathered(0)
    p2a = [
        (
            send(ss.at[h, 0, pl.ds(0, 64)], ra2.at[h, 0], step[1 - h](1)),
            send(ss.at[h, 0, pl.ds(64, 64)], ra2.at[h, 1], step[1 - h](-1)),
        )
        for h in range(2)
    ]
    load_w.wait()
    for h in range(2):
        for d1 in range(4):
            for c in g_b2[h, d1]:
                c.wait_recv()
    share_w = [
        send(wr.at[dy, :, core], wr.at[dy, :, core], dev(dc=1)) for dy in range(4)
    ]

    act_rows(0)

    gathered(1)
    def last(src, h, s, c):
        return send(src, rx2.at[core, h, s], step[1 - h](1 - 2 * s, c), wsem.at[core, h, s])

    for h in range(2):
        last(ss.at[h, 1, pl.ds(64, 64)], h, 0, 1)
        last(ss.at[h, 2, pl.ds(0, 64)], h, 1, 0)
    for h in range(2):
        for s in range(2):
            p2a[h][s].wait_recv()
            cb2[h, s] = ss[h, 1 + s, 64 * s : 64 * s + 64] + ra2[h, s]
            last(cb2.at[h, s], h, s, s)

    send_c(2)
    act_rows(1)
    act_rows(2)
    act_rows(3)
    store = pltpu.make_async_copy(act_v, act_out, lsem.at[4])
    store.start()

    gathered(2)
    given = [
        send(ss.at[h, 3, pl.ds(pl.multiple_of(64 * (1 - core), 64), 64)], wsw.at[h], dev(dc=1))
        for h in range(2)
    ]
    for h in range(2):
        given[h].wait_recv()
    for c in range(2):
        for h in range(2):
            for s in range(2):
                pltpu.make_async_remote_copy(
                    src_ref=cb2.at[h, s], dst_ref=rx2.at[c, h, s], send_sem=ssem.at[0],
                    recv_sem=wsem.at[c, h, s], device_id=dev(dc=1), device_id_type=MESH,
                ).wait_recv()
    mine = pl.ds(pl.multiple_of(64 * core, 64), 64)
    for h in range(2):
        near = pl.ds(pl.multiple_of(256 * core + 128 * h, 128), 128)
        far = pl.ds(pl.multiple_of(256 * (1 - core) + 128 * h, 128), 128)
        wg_out[:, near] = ss[h, 3, mine] + rx2[core, h, 0] + rx2[core, h, 1]
        wg_out[:, far] = wsw[h] + rx2[1 - core, h, 0] + rx2[1 - core, h, 1]
    store.wait()
    assert len(started) == N_SEMS
    for c in started:
        c.wait_send()


def finish(act_in, wg_in, act_out, wg_out, act_v, wg_v, sems):
    parts = [(wg_in, wg_v, wg_out)]
    for k in range(8):
        rows = pl.ds(64 * k, 64)
        parts.append((act_in.at[rows], act_v.at[rows], act_out.at[rows]))
    loads = [pltpu.make_async_copy(a, b, sems.at[0, k]) for k, (a, b, _) in enumerate(parts)]
    stores = [pltpu.make_async_copy(b, c, sems.at[1, k]) for k, (_, b, c) in enumerate(parts)]
    for c in loads:
        c.start()
    for c, d in zip(loads, stores):
        c.wait()
        d.start()
    for d in stores:
        d.wait()


def shards(acts, key_grads, key_weight, lengths, threshold):
    hbm = pl.BlockSpec(memory_space=pltpu.HBM)
    anywhere = pl.BlockSpec(memory_space=pl.ANY)
    smem = pl.BlockSpec(memory_space=pltpu.SMEM)
    v = pltpu.VMEM
    act_part, weight_part = pl.pallas_call(
        kernel,
        out_shape=(
            jax.ShapeDtypeStruct((TOK, D), BF16),
            jax.ShapeDtypeStruct((D // 32, KV), F32),
        ),
        in_specs=[hbm, hbm, hbm, smem, smem],
        out_specs=(anywhere, pl.BlockSpec(memory_space=v)),
        scratch_shapes=[
            v((2, TOK, D), BF16),
            v((TOK, KV), BF16),
            v((TOK, 256), BF16),
            v((256, 2 * TOK), BF16),
            v((256, 2 * TOK), BF16),
            v((4, 4, 2, 64, KV), BF16),
            v((TOK, D), BF16),
            v((1, TOK), F32),
            v((15, 1, TOK), F32),
            v((1, TOK), F32),
            v((1, TOK), F32),
            v((2, 3, 4, 128, 128), BF16),
            v((2, 2, 4, 64, 128), F32),
            v((2, 4, 128, 128), F32),
            v((2, 2, 4, 64, 128), BF16),
            v((2, 2, 4, 64, 128), BF16),
            v((2, 2, 4, 128, 128), BF16),
            v((2, 4, 128, 128), F32),
            v((2, 2, 64, 128), F32),
            v((2, 2, 64, 128), F32),
            v((2, 2, 2, 64, 128), F32),
            v((2, 64, 128), F32),
            pltpu.SemaphoreType.DMA((N_SEMS,)),
            pltpu.SemaphoreType.DMA((N_SEMS,)),
            pltpu.SemaphoreType.DMA((2, 2, 2)),
            pltpu.SemaphoreType.DMA((5,)),
        ],
        compiler_params=pltpu.CompilerParams(
            collective_id=0, has_side_effects=True, vmem_limit_bytes=VMEM
        ),
    )(acts[0], key_grads[0], key_weight[0], lengths, threshold.reshape(1, 1))
    act_part, weight_part = pl.pallas_call(
        finish,
        out_shape=(
            jax.ShapeDtypeStruct((TOK, D), BF16),
            jax.ShapeDtypeStruct((D // 32, KV), F32),
        ),
        in_specs=[hbm, hbm],
        out_specs=(hbm, hbm),
        scratch_shapes=[v((TOK, D), BF16), v((D // 32, KV), F32), pltpu.SemaphoreType.DMA((2, 9))],
        compiler_params=pltpu.CompilerParams(vmem_limit_bytes=VMEM),
    )(act_part, weight_part)
    return (act_part[None], weight_part[None])


def solution(mesh):
    in_specs = (
        P("section", "dp", None),
        P("section", "dp", None),
        P("section", "dp", None),
        P("dp", None),
        P(),
    )
    out_specs = (P("section", "dp", None), P("section", "dp", None))
    return jax.shard_map(shards, mesh=mesh, in_specs=in_specs, out_specs=out_specs, check_vma=False)
```
